128 devices in a mesh: ctx: 32 (over x, y, core), head: 4 (over z).
Axes of the slice: x: 4, y: 4, z: 4, core: 2. Of those that a mesh axis runs over, the one named last changes fastest.
Arguments:
- queries: bfloat16 [32768, 2048], P('ctx', 'head'), may hold values from -80 to 80
- row_keys: bfloat16 [32768, 128], P('ctx'), may hold values from -4 to 4
- row_values: bfloat16 [32768, 128], P('ctx'), may hold values from -12 to 12
- cached_keys: bfloat16 [4096, 128], P('ctx'), may hold values from -4 to 4
- cached_values: bfloat16 [4096, 128], P('ctx'), may hold values from -12 to 12
- doc_ids: int32 [32768], replicated, may hold values from 0 to 31, never falling along the last dimension, each value on 1 to 4096 neighbouring positions
- prefix_lens: int32 [32], replicated, may hold values from 1 to 512, 4096 in all
- block_order: int32 [256], replicated, may hold values from 0 to 255, each once
- out_weight: bfloat16 [2048, 4096], P('head'), may hold values from -0.25 to 0.25
Outputs:
- mixed: bfloat16 [32768, 4096], P('ctx', 'head')
The draws below stay inside these ranges and needn't reach their ends.
Inputs may be any that keep to these rules, and one draw needn't show every extreme that they name: `doc_ids`: row positions in row order; numbers never fall; each document has 1 to 4096 positions. `prefix_lens`: the lengths sum to 4096; cached rows hold the documents' prefixes in document order. `block_order`: each row block stands in exactly one slot block.
All inputs are finite; a program needn't handle non-finite values.
Results may differ from the reference program's by a relative error of at most 0.017.
Values may be sent and summed in bfloat16 or wider, within the bound.
No kernel may reach another device: no remote copies, remote signals or barrier semaphores. Data moves between devices by JAX's collectives and lax.ppermute only.
A program may use at most 128 MiB of HBM per device.

```python
import math
import jax
import jax.numpy as jnp
import numpy as np
from jax import lax

DM = 4096
HD = 128
QHEADS = 16
BLK = 128
TOKENS = 32768
PTOKENS = 4096
NBLK = 256
NDOC = 32
DOC_MOST = 4096
PMOST = 512


def shared_keys(key):
    base = jnp.clip(jax.random.normal(key, (TOKENS, HD), jnp.float32), -4.0, 4.0)
    return base


def draw_queries(key, part):
    key = jax.random.fold_in(key, 3)
    values = jnp.clip(jax.random.normal(key, (TOKENS, QHEADS, HD), jnp.float32), -4.0, 4.0)
    return values.reshape(TOKENS, QHEADS * HD).astype(jnp.bfloat16)


def draw_row_keys(key, part):
    base = shared_keys(key)
    values = base
    return values.astype(jnp.bfloat16)


def block_levels(own_key, dims, split, low, high):
    def one(dim, shards_of):
        draws = jax.random.uniform(jax.random.fold_in(jax.random.fold_in(own_key, 6), dim), (shards_of,), jnp.float32, low / len(split), high / len(split))
        return jnp.repeat(jnp.exp(draws), dims[dim] // shards_of).reshape((-1,) + (1,) * (len(dims) - dim - 1))

    factor_of = one(*split[0])
    for cut in split[1:]:
        factor_of = factor_of * one(*cut)
    return factor_of


def profile(count, total, reach, lean):
    portions = [(1 << 20) // math.isqrt(rank ** lean) + 1 for rank in range(2, count + 1)]
    surplus, given = total - reach - (count - 1), [1] * (count - 1)
    while surplus > 0:
        movable = [i for i in range(count - 1) if given[i] < reach]
        pool, remaining = sum([portions[i] for i in movable]), surplus
        for i in movable:
            addition = min(reach - given[i], max(1, remaining * portions[i] // pool), surplus)
            given[i] = given[i] + addition
            surplus = surplus - addition
    return np.array([reach] + given)


def ragged_sizes(stream_key, amount, total, limit, lean):
    if amount == 2:
        one = jax.random.randint(stream_key, (), max(1, total - limit), min(limit, total - 1) + 1)
        return jnp.stack([one, total - one])
    sizes = jnp.asarray(profile(amount, total, limit, lean), jnp.int32)
    pairs = (amount - 1) // 2
    giver, receiver = sizes[1:1 + 2 * pairs:2], sizes[2:2 + 2 * pairs:2]
    room = jnp.minimum(giver - 1, limit - receiver)
    moved = jax.random.randint(jax.random.fold_in(stream_key, 1), (pairs,), 0, 1 << 20) % (room + 1)
    sizes = sizes.at[1:1 + 2 * pairs:2].set(giver - moved).at[2:2 + 2 * pairs:2].set(receiver + moved)
    return sizes[jax.random.permutation(jax.random.fold_in(stream_key, 2), amount)]


def scatter_about(own_key, dims, width, reach, cuts=(), kind=jnp.bfloat16):
    entries = jax.random.normal(own_key, dims, jnp.float32) * width
    if len(cuts) > 0:
        entries = block_levels(own_key, dims, cuts, -0.22, 0.18) * entries
    return jnp.clip(entries, min=-reach, max=reach).astype(kind)


def setup_inputs(seed: int = 0) -> dict:
    key_of = jax.random.split(jax.random.key(seed), 10)
    return {
        "queries": draw_queries(jax.random.fold_in(key_of[9], 71), 0),
        "row_keys": draw_row_keys(jax.random.fold_in(key_of[9], 71), 0),
        "row_values": scatter_about(key_of[2], (TOKENS, HD), 3.0, 12.0, ((0, 32),)),
        "cached_keys": scatter_about(key_of[3], (PTOKENS, HD), 1.0, 4.0, ((0, 32),)),
        "cached_values": scatter_about(key_of[4], (PTOKENS, HD), 3.0, 12.0, ((0, 32),)),
        "doc_ids": jnp.searchsorted(jnp.cumsum(ragged_sizes(key_of[5], NDOC, TOKENS, DOC_MOST, 2)), jnp.arange(TOKENS), side="right").astype(jnp.int32),
        "prefix_lens": ragged_sizes(key_of[6], NDOC, PTOKENS, PMOST, 2).astype(jnp.int32),
        "block_order": jax.random.permutation(key_of[7], NBLK).astype(jnp.int32),
        "out_weight": scatter_about(key_of[8], (QHEADS * HD, DM), (QHEADS * HD // 4) ** -0.5, 0.25, ((0, 4),)),
    }


NEG = -1.0e30


def reference(queries, row_keys, row_values, cached_keys, cached_values, doc_ids, prefix_lens, block_order, out_weight):
    heads = queries.shape[1] // HD
    scale = 1.0 / (HD ** 0.5)
    inverse = jnp.argsort(block_order).astype(jnp.int32)
    key_rows = row_keys.reshape(NBLK, BLK, HD)[inverse].reshape(TOKENS, HD).astype(jnp.float32)
    value_rows = row_values.reshape(NBLK, BLK, HD)[inverse].reshape(TOKENS, HD).astype(jnp.float32)
    cached_k = cached_keys.astype(jnp.float32)
    cached_v = cached_values.astype(jnp.float32)
    prefix_end = jnp.cumsum(prefix_lens).astype(jnp.int32)
    cached_index = jnp.arange(PTOKENS, dtype=jnp.int32)
    cached_doc = jnp.sum((prefix_end[None, :] <= cached_index[:, None]).astype(jnp.int32), axis=1).astype(jnp.int32)
    window = DOC_MOST + BLK
    query_blocks = queries.reshape(NBLK, BLK, heads, HD)

    def one_block(inputs):
        query_block, row_block = inputs
        first = (row_block * BLK).astype(jnp.int32)
        query_pos = first + jnp.arange(BLK, dtype=jnp.int32)
        query_doc = lax.dynamic_slice_in_dim(doc_ids, first, BLK, 0)
        start = jnp.maximum(first + BLK - window, 0).astype(jnp.int32)
        window_k = lax.dynamic_slice_in_dim(key_rows, start, window, 0)
        window_v = lax.dynamic_slice_in_dim(value_rows, start, window, 0)
        key_pos = start + jnp.arange(window, dtype=jnp.int32)
        key_doc = lax.dynamic_slice_in_dim(doc_ids, start, window, 0)
        row_mask = (key_doc[None, :] == query_doc[:, None]) & (key_pos[None, :] <= query_pos[:, None])
        cached_mask = cached_doc[None, :] == query_doc[:, None]
        query_f = query_block.astype(jnp.float32)
        row_score = jnp.einsum("qhd,kd->hqk", query_f, window_k) * scale
        cached_score = jnp.einsum("qhd,kd->hqk", query_f, cached_k) * scale
        row_score = jnp.where(row_mask[None], row_score, NEG)
        cached_score = jnp.where(cached_mask[None], cached_score, NEG)
        top = jnp.maximum(jnp.max(row_score, axis=-1), jnp.max(cached_score, axis=-1))
        row_weight = jnp.where(row_mask[None], jnp.exp(row_score - top[..., None]), 0.0)
        cached_weight = jnp.where(cached_mask[None], jnp.exp(cached_score - top[..., None]), 0.0)
        total = jnp.sum(row_weight, axis=-1) + jnp.sum(cached_weight, axis=-1)
        row_round = lax.optimization_barrier(row_weight.astype(jnp.bfloat16)).astype(jnp.float32)
        cached_round = lax.optimization_barrier(cached_weight.astype(jnp.bfloat16)).astype(jnp.float32)
        summed = jnp.einsum("hqk,kd->hqd", row_round, window_v) + jnp.einsum("hqk,kd->hqd", cached_round, cached_v)
        result = summed / total[..., None]
        return jnp.transpose(result, (1, 0, 2)).reshape(BLK, heads * HD).astype(jnp.bfloat16)

    attended = lax.map(one_block, (query_blocks, block_order)).reshape(TOKENS, heads * HD)
    return jnp.dot(attended, out_weight, preferred_element_type=jnp.float32).astype(jnp.bfloat16)
```

```python
import functools

import jax
import jax.numpy as jnp
from jax import lax
from jax.experimental import pallas as pl
from jax.experimental.pallas import tpu as pltpu
from jax.sharding import PartitionSpec as P

BLK = 128
UNSEEN = -2e30
LOWEST = -1e30
FAR = 1 << 24


def attend_kernel(
    scale, heads, order_ref, count_ref, base_ref, bounds_ref, q_ref, kv_ref, out_ref, qt_ref, acc_ref, top_ref
):
    blocks = q_ref.shape[0] // BLK
    size = q_ref.shape[1] // heads
    wide = heads * BLK
    half = wide // 2
    row_span = base_ref.shape[0] // 9 * 8 * BLK
    ones = jnp.ones((16, 2 * BLK), jnp.bfloat16)
    key_row = lax.broadcasted_iota(jnp.int32, (BLK, half), 0)

    def one_block(j, _):
        rows = pl.ds(pl.multiple_of(j * BLK, BLK), BLK)
        for h in range(heads):
            qt_ref[:, h * BLK : (h + 1) * BLK] = q_ref[rows, h * size : (h + 1) * size].T
        top_ref[...] = jnp.full(top_ref.shape, LOWEST, jnp.float32)
        acc_ref[...] = jnp.zeros(acc_ref.shape, jnp.float32)
        full = count_ref[j, 0] // 2
        seen = count_ref[j, 1]

        def tile(t, masked):
            first, second = order_ref[j, 2 * t], order_ref[j, 2 * t + 1]
            one, two = kv_ref[first], kv_ref[second]
            keys = jnp.concatenate([one[:, :size], two[:, :size]], axis=0)
            values = jnp.concatenate([one[:, size:], two[:, size:]], axis=1)
            values = jnp.concatenate([values, ones], axis=0)
            for part in range(2):
                cols = slice(part * half, (part + 1) * half)
                score = jnp.dot(keys, qt_ref[:, cols], preferred_element_type=jnp.float32)
                if masked:
                    pieces = []
                    for n, index in enumerate((first, second)):
                        base = jnp.where(2 * t + n < seen, base_ref[index], FAR)
                        cached = base >= row_span
                        low = jnp.where(cached, bounds_ref[j, 2:3, cols], bounds_ref[j, 0:1, cols])
                        high = jnp.where(cached, bounds_ref[j, 3:4, cols], bounds_ref[j, 1:2, cols])
                        row = key_row + base
                        piece = score[n * BLK : (n + 1) * BLK]
                        pieces.append(jnp.where((row >= low) & (row <= high), piece, UNSEEN))
                    score = jnp.concatenate(pieces, axis=0)
                old = top_ref[0:1, cols]
                new = jnp.maximum(old, jnp.max(score, axis=0, keepdims=True))
                weight = jnp.exp2(score * scale - new * scale).astype(jnp.bfloat16)
                factor = jnp.exp2((old - new) * scale)
                top_ref[0:1, cols] = new
                acc_ref[:, cols] = acc_ref[:, cols] * factor + jnp.dot(
                    values, weight, preferred_element_type=jnp.float32
                )

        def plain(t, _):
            tile(t, False)
            return 0

        def edge(t, _):
            tile(t, True)
            return 0

        lax.fori_loop(0, full, plain, 0)
        lax.fori_loop(full, (seen + 1) // 2, edge, 0)
        for h in range(heads):
            cols = slice(h * BLK, (h + 1) * BLK)
            result = acc_ref[:size, cols] / acc_ref[size : size + 1, cols]
            out_ref[rows, h * size : (h + 1) * size] = result.T.astype(out_ref.dtype)
        return 0

    lax.fori_loop(0, blocks, one_block, 0)


def attend(queries, kv, order, count, base, bounds, heads, size):
    wide = heads * BLK
    scale = 1.4426950408889634 / size**0.5
    smem = pl.BlockSpec(memory_space=pltpu.SMEM)
    vmem = pl.BlockSpec(memory_space=pltpu.VMEM)
    return pl.pallas_call(
        functools.partial(attend_kernel, scale, heads),
        out_shape=jax.ShapeDtypeStruct(queries.shape, jnp.bfloat16),
        in_specs=[smem, smem, smem, vmem, vmem, vmem],
        out_specs=vmem,
        scratch_shapes=[
            pltpu.VMEM((size, wide), jnp.bfloat16),
            pltpu.VMEM((size + 16, wide), jnp.float32),
            pltpu.VMEM((8, wide), jnp.float32),
        ],
        compiler_params=pltpu.CompilerParams(vmem_limit_bytes=48 << 20),
        cost_estimate=pl.CostEstimate(flops=8 << 30, bytes_accessed=24 << 20, transcendentals=8 << 20),
        name="attend",
    )(order, count, base, bounds, queries, kv)


def plan(doc_ids, prefix_lens, block_order, shard_index, local_blocks, shards, heads):
    block_count = block_order.shape[0]
    rows = doc_ids.shape[0]
    inside = jnp.arange(BLK, dtype=jnp.int32)
    mine = lax.dynamic_slice_in_dim(block_order, shard_index * local_blocks, local_blocks, 0)
    doc = doc_ids.reshape(block_count, BLK)[mine]
    position = mine[:, None] * BLK + inside[None, :]
    docs = jnp.arange(prefix_lens.shape[0], dtype=jnp.int32)
    doc_start = jnp.sum((doc_ids[None, :] < docs[:, None]).astype(jnp.int32), axis=1)
    prefix_end = jnp.cumsum(prefix_lens)
    prefix_start = prefix_end - prefix_lens
    chosen = doc[:, :, None] == docs[None, None, :]
    pick = lambda table: jnp.sum(jnp.where(chosen, table[None, None, :], 0), axis=2)
    low_row, high_row = pick(doc_start), position
    low_cached, high_cached = pick(prefix_start) + rows, pick(prefix_end) + (rows - 1)
    bounds = jnp.stack([low_row, high_row, low_cached, high_cached], axis=1)
    bounds = jnp.tile(bounds, (1, 2, heads)).astype(jnp.int32)
    row_base = block_order.reshape(shards, local_blocks) * BLK
    cached_base = rows + jnp.arange(shards, dtype=jnp.int32)[:, None] * BLK
    base = jnp.concatenate([row_base, cached_base], axis=1).reshape(-1)
    index = jnp.arange(base.shape[0], dtype=jnp.int32)
    cached = (base >= rows)[None, :]
    ends = lambda array, at: array[:, at][:, None]
    first = base[None, :]
    last = first + (BLK - 1)
    seen = jnp.where(
        cached,
        (last >= ends(low_cached, 0)) & (first <= ends(high_cached, -1)),
        (last >= ends(low_row, 0)) & (first <= ends(high_row, -1)),
    )
    whole = jnp.where(
        cached,
        (first >= ends(low_cached, -1)) & (last <= ends(high_cached, 0)),
        (first >= ends(low_row, -1)) & (last <= ends(high_row, 0)),
    )
    key = jnp.where(whole, index[None, :], jnp.where(seen, 1024 + index[None, :], 4096 + index[None, :]))
    order = jnp.sort(key, axis=1) % 1024
    count = jnp.stack([jnp.sum(whole, axis=1), jnp.sum(seen, axis=1)], axis=1).astype(jnp.int32)
    return order, count, base, bounds


def on_device(
    queries,
    row_keys,
    row_values,
    cached_keys,
    cached_values,
    doc_ids,
    prefix_lens,
    block_order,
    out_weight,
):
    size = row_keys.shape[1]
    heads = queries.shape[1] // size
    local_blocks = queries.shape[0] // BLK
    shards = lax.axis_size("ctx")
    keys = jnp.concatenate([row_keys, cached_keys], axis=0).reshape(-1, BLK, size)
    values = jnp.concatenate([row_values, cached_values], axis=0).reshape(-1, BLK, size)
    packed = jnp.concatenate([keys, jnp.swapaxes(values, 1, 2)], axis=2)
    gathered = lax.all_gather(packed, "ctx", axis=0, tiled=True)
    weight = lax.all_to_all(out_weight, "head", 1, 0, tiled=True)
    order, count, base, bounds = plan(
        doc_ids, prefix_lens, block_order, lax.axis_index("ctx"), local_blocks, shards, heads
    )
    gathered, weight = lax.optimization_barrier((gathered, weight))
    attended = attend(queries, gathered, order, count, base, bounds, heads, size)
    attended = lax.all_gather(attended, "head", axis=1, tiled=True)
    return jnp.dot(attended, weight, preferred_element_type=jnp.float32).astype(jnp.bfloat16)


def solution(mesh):
    placed = (
        P("ctx", "head"),
        P("ctx", None),
        P("ctx", None),
        P("ctx", None),
        P("ctx", None),
        P(),
        P(),
        P(),
        P("head", None),
    )
    return jax.shard_map(
        on_device, mesh=mesh, in_specs=placed, out_specs=P("ctx", "head"), check_vma=False
    )
```

```python
import functools

import jax
import jax.numpy as jnp
from jax import lax
from jax.experimental import pallas as pl
from jax.experimental.pallas import tpu as pltpu
from jax.sharding import Mesh
from jax.sharding import PartitionSpec as P

BLK = 128
TILE = 4
UNSEEN = -2e30
LOWEST = -1e30
FAR = 1 << 24
CTX = ("x", "y", "core")


def attend_kernel(scale, row_span, first_stage, last_stage, begin, blocks, pieces, *refs):
    order_ref, count_ref, base_ref, bounds_ref, qt_ref = refs[:5]
    refs = refs[5:]
    piece_refs, refs = refs[:pieces], refs[pieces:]
    if not first_stage:
        acc_in, top_in, *refs = refs
    if last_stage:
        out_ref, *refs = refs
    else:
        acc_out, top_out, *refs = refs
    kv_ref, acc_ref, top_ref, score_a, score_b, tile_row, tile_first, tile_kind, sems = refs
    size = qt_ref.shape[1]
    wide = qt_ref.shape[2]
    half = wide // 2
    heads = wide // BLK
    depth = TILE * BLK
    span = acc_ref.shape[1]

    copies = []
    at = 0
    for n, piece in enumerate(piece_refs):
        count = piece.shape[0]
        copies.append(pltpu.make_async_copy(piece, kv_ref.at[pl.ds(at, count)], sems.at[n]))
        at += count
    if not first_stage:
        copies.append(pltpu.make_async_copy(acc_in.at[pl.ds(begin, blocks)], acc_ref, sems.at[pieces]))
        copies.append(pltpu.make_async_copy(top_in.at[pl.ds(begin, blocks)], top_ref, sems.at[pieces + 1]))
    for copy in copies:
        copy.start()
    if first_stage:
        acc_ref[...] = jnp.zeros(acc_ref.shape, jnp.float32)
        top_ref[...] = jnp.full(top_ref.shape, LOWEST, jnp.float32)

    def list_row(j, t):
        whole, seen = count_ref[begin + j, 0], count_ref[begin + j, 1]

        def list_tile(i, t):
            tile_row[t] = j
            tile_first[t] = i * TILE
            tile_kind[t] = jnp.where(i * TILE + TILE <= whole, TILE + 1, jnp.minimum(seen - i * TILE, TILE))
            return t + 1

        return lax.fori_loop(0, (seen + (TILE - 1)) // TILE, list_tile, t)

    tiles = lax.fori_loop(0, blocks, list_row, 0)
    for n in range(2):
        tile_row[tiles + n] = 0
        tile_first[tiles + n] = 0
        tile_kind[tiles + n] = 0
    for copy in copies:
        copy.wait()

    ones = jnp.ones((span - size, depth), jnp.bfloat16)
    key_row = lax.broadcasted_iota(jnp.int32, (BLK, half), 0)

    def indices(t):
        j, first = tile_row[t] + begin, tile_first[t]
        return [order_ref[j, first + n] for n in range(TILE)]

    def score(t, score_ref):
        keys = jnp.concatenate([kv_ref[index, :, :size] for index in indices(t)], axis=0)
        j = tile_row[t] + begin
        for part in range(2):
            cols = slice(part * half, (part + 1) * half)
            score_ref[:, cols] = jnp.dot(keys, qt_ref[j, :, cols], preferred_element_type=jnp.float32)

    def fold(t, score_ref, masked):
        picked = indices(t)
        values = jnp.concatenate([kv_ref[index, :, size:] for index in picked], axis=1)
        values = jnp.concatenate([values, ones], axis=0)
        j = tile_row[t]
        kind = tile_kind[t]
        for part in range(2):
            cols = slice(part * half, (part + 1) * half)
            if masked:
                shown = []
                for n, index in enumerate(picked):
                    base = jnp.where(n < kind, base_ref[index], FAR)
                    cached = base >= row_span
                    low = jnp.where(cached, bounds_ref[begin + j, 2:3, cols], bounds_ref[begin + j, 0:1, cols])
                    high = jnp.where(cached, bounds_ref[begin + j, 3:4, cols], bounds_ref[begin + j, 1:2, cols])
                    row = key_row + base
                    piece = score_ref[n * BLK : (n + 1) * BLK, cols]
                    shown.append(jnp.where((row >= low) & (row <= high), piece, UNSEEN))
                scores = jnp.concatenate(shown, axis=0)
            else:
                scores = score_ref[:, cols]
            old = top_ref[j, 0:1, cols]
            new = jnp.maximum(old, jnp.max(scores, axis=0, keepdims=True))
            weight = jnp.exp2(scores * scale - new * scale).astype(jnp.bfloat16)
            factor = jnp.exp2((old - new) * scale)
            top_ref[j, 0:1, cols] = new
            acc_ref[j, :, cols] = acc_ref[j, :, cols] * factor + jnp.dot(
                values, weight, preferred_element_type=jnp.float32
            )

    def step(t, here, there):
        plain = tile_kind[t] > TILE

        @pl.when(plain)
        def _():
            score(t + 1, there)
            fold(t, here, False)

        @pl.when(jnp.logical_not(plain))
        def _():
            score(t + 1, there)
            fold(t, here, True)

    def pair(i, _):
        step(2 * i, score_a, score_b)
        step(2 * i + 1, score_b, score_a)
        return 0

    @pl.when(tiles > 0)
    def _():
        score(0, score_a)
        lax.fori_loop(0, (tiles + 1) // 2, pair, 0)

    if last_stage:

        def finish(j, _):
            rows = pl.ds(pl.multiple_of(j * BLK, BLK), BLK)
            for h in range(heads):
                cols = slice(h * BLK, (h + 1) * BLK)
                result = acc_ref[j, :size, cols] / acc_ref[j, size : size + 1, cols]
                out_ref[rows, h * size : (h + 1) * size] = result.T.astype(out_ref.dtype)
            return 0

        lax.fori_loop(0, blocks, finish, 0)
    else:
        back = [
            pltpu.make_async_copy(acc_ref, acc_out, sems.at[0]),
            pltpu.make_async_copy(top_ref, top_out, sems.at[1]),
        ]
        for copy in back:
            copy.start()
        for copy in back:
            copy.wait()


def attend(qt, pieces, stage, bounds, state, row_span, name, begin=0, blocks=None, last_stage=False):
    order, count, base = stage
    total, size, wide = qt.shape
    blocks = total if blocks is None else blocks
    first_stage = state is None
    scale = 1.4426950408889634 / size**0.5
    span = size + 16
    smem = pl.BlockSpec(memory_space=pltpu.SMEM)
    vmem = pl.BlockSpec(memory_space=pltpu.VMEM)
    hbm = pl.BlockSpec(memory_space=pl.ANY)
    held = sum(piece.shape[0] for piece in pieces)
    tiles = blocks * (held // TILE) + 2
    if last_stage:
        out_shape = jax.ShapeDtypeStruct((blocks * BLK, wide // BLK * size), jnp.bfloat16)
        out_specs = vmem
    else:
        out_shape = (
            jax.ShapeDtypeStruct((total, span, wide), jnp.float32),
            jax.ShapeDtypeStruct((total, 8, wide), jnp.float32),
        )
        out_specs = (hbm, hbm)
    return pl.pallas_call(
        functools.partial(
            attend_kernel, scale, row_span, first_stage, last_stage, begin, blocks, len(pieces)
        ),
        out_shape=out_shape,
        in_specs=[smem, smem, smem, vmem, vmem] + [hbm] * len(pieces) + [hbm] * (0 if first_stage else 2),
        out_specs=out_specs,
        scratch_shapes=[
            pltpu.VMEM((held, BLK, 2 * size), jnp.bfloat16),
            pltpu.VMEM((blocks, span, wide), jnp.float32),
            pltpu.VMEM((blocks, 8, wide), jnp.float32),
            pltpu.VMEM((TILE * BLK, wide), jnp.float32),
            pltpu.VMEM((TILE * BLK, wide), jnp.float32),
            pltpu.SMEM((tiles,), jnp.int32),
            pltpu.SMEM((tiles,), jnp.int32),
            pltpu.SMEM((tiles,), jnp.int32),
            pltpu.SemaphoreType.DMA((len(pieces) + 2,)),
        ],
        compiler_params=pltpu.CompilerParams(vmem_limit_bytes=56 << 20),
        cost_estimate=pl.CostEstimate(flops=2 << 30, bytes_accessed=8 << 20, transcendentals=2 << 20),
        name=name,
    )(order, count, base, bounds, qt, *pieces, *(() if first_stage else state))


def plan(doc_ids, prefix_lens, block_order, mine, stage_bases, heads):
    block_count = block_order.shape[0]
    rows = doc_ids.shape[0]
    inside = jnp.arange(BLK, dtype=jnp.int32)
    doc = doc_ids.reshape(block_count, BLK)[mine]
    position = mine[:, None] * BLK + inside[None, :]
    docs = jnp.arange(prefix_lens.shape[0], dtype=jnp.int32)
    doc_start = jnp.sum((doc_ids[None, :] < docs[:, None]).astype(jnp.int32), axis=1)
    prefix_end = jnp.cumsum(prefix_lens)
    prefix_start = prefix_end - prefix_lens
    chosen = doc[:, :, None] == docs[None, None, :]
    pick = lambda table: jnp.sum(jnp.where(chosen, table[None, None, :], 0), axis=2)
    low_row, high_row = pick(doc_start), position
    low_cached, high_cached = pick(prefix_start) + rows, pick(prefix_end) + (rows - 1)
    bounds = jnp.stack([low_row, high_row, low_cached, high_cached], axis=1)
    bounds = jnp.tile(bounds, (1, 2, heads)).astype(jnp.int32)
    width = max(base.shape[0] for base in stage_bases)
    fill = lambda base: jnp.pad(base, (0, width - base.shape[0]), constant_values=FAR)
    first = jnp.stack([fill(base) for base in stage_bases])[:, None, :]
    last = first + (BLK - 1)
    cached = first >= rows
    ends = lambda array, at: array[:, at][None, :, None]
    seen = jnp.where(
        cached,
        (last >= ends(low_cached, 0)) & (first <= ends(high_cached, -1)),
        (last >= ends(low_row, 0)) & (first <= ends(high_row, -1)),
    )
    whole = jnp.where(
        cached,
        (first >= ends(low_cached, -1)) & (last <= ends(high_cached, 0)),
        (first >= ends(low_row, -1)) & (last <= ends(high_row, 0)),
    )
    index = jnp.arange(width, dtype=jnp.int32)[None, None, :]
    key = jnp.where(whole, index, jnp.where(seen, 1024 + index, 4096 + index))
    order = lax.sort(key, dimension=2) % 1024
    count = jnp.stack([jnp.sum(whole, axis=2), jnp.sum(seen, axis=2)], axis=2).astype(jnp.int32)
    return [(order[n, :, : base.shape[0]], count[n], base) for n, base in enumerate(stage_bases)], bounds


def on_device(
    queries,
    row_keys,
    row_values,
    cached_keys,
    cached_values,
    doc_ids,
    prefix_lens,
    block_order,
    out_weight,
):
    size = row_keys.shape[1]
    heads = queries.shape[1] // size
    local_blocks = queries.shape[0] // BLK
    n_x, n_y, n_z = lax.axis_size("x"), lax.axis_size("y"), lax.axis_size("z")
    x, y, core, z = (lax.axis_index(axis) for axis in ("x", "y", "core", "z"))
    rows = doc_ids.shape[0]

    along_z = lambda array, shift: lax.ppermute(array, "z", [(i, (i + shift) % n_z) for i in range(n_z)])

    def pack(keys, values):
        keys, values = keys.reshape(-1, BLK, size), values.reshape(-1, BLK, size)
        return jnp.concatenate([keys, jnp.swapaxes(values, 1, 2)], axis=2)

    packed = jnp.concatenate([pack(row_keys, row_values), pack(cached_keys, cached_values)], axis=0)
    gathered = lax.all_gather(packed, CTX, axis=0, tiled=True)
    columns = out_weight.shape[1] // n_z
    weight_for = lambda shift: lax.dynamic_slice_in_dim(out_weight, ((z + shift) % n_z) * columns, columns, 1)
    weight = jnp.concatenate([weight_for(0)] + [along_z(weight_for(s), s) for s in (1, -1, 2)], axis=0)

    shards = n_x * n_y * 2
    row_base = block_order.reshape(shards, local_blocks) * BLK
    cached_base = rows + jnp.arange(shards, dtype=jnp.int32)[:, None] * BLK
    stage_bases = [jnp.concatenate([row_base, cached_base], axis=1).reshape(-1)]
    shard = (x * n_y + y) * 2 + core
    mine = lax.dynamic_slice_in_dim(block_order, shard * local_blocks, local_blocks, 0)
    stages, bounds = plan(doc_ids, prefix_lens, block_order, mine, stage_bases, heads)
    qt = jnp.transpose(queries.reshape(local_blocks, BLK, heads, size), (0, 3, 2, 1))
    qt = qt.reshape(local_blocks, size, heads * BLK)
    gathered, weight, qt, stages, bounds = lax.optimization_barrier((gathered, weight, qt, stages, bounds))
    part_blocks = local_blocks // 2
    part_rows = part_blocks * BLK
    outs = []
    for part in range(2):
        mine = attend(
            qt,
            (gathered,),
            stages[0],
            bounds,
            None,
            rows,
            "attend_part",
            begin=part * part_blocks,
            blocks=part_blocks,
            last_stage=True,
        )
        below, above = along_z(mine, 1), along_z(mine, -1)
        opposite = jnp.concatenate(
            [along_z(below[: part_rows // 2], 1), along_z(above[part_rows // 2 :], -1)], axis=0
        )
        every = jnp.concatenate([mine, below, above, opposite], axis=1)
        outs.append(jnp.dot(every, weight, preferred_element_type=jnp.float32).astype(jnp.bfloat16))
    return jnp.concatenate(outs, axis=0)


def solution(mesh):
    grid = Mesh(mesh.devices.reshape(4, 4, 2, mesh.shape["head"]), ("x", "y", "core", "z"))
    placed = (
        P(CTX, "z"),
        P(CTX, None),
        P(CTX, None),
        P(CTX, None),
        P(CTX, None),
        P(),
        P(),
        P(),
        P("z", None),
    )
    return jax.shard_map(
        on_device, mesh=grid, in_specs=placed, out_specs=P(CTX, "z"), check_vma=False
    )
```

```python
import functools

import jax
import jax.numpy as jnp
from jax import lax
from jax.experimental import pallas as pl
from jax.experimental.pallas import tpu as pltpu
from jax.sharding import Mesh
from jax.sharding import PartitionSpec as P

BLK = 128
TILE = 4
UNSEEN = -2e30
LOWEST = -1e30
FAR = 1 << 24
CTX = ("x", "y", "core")


def pack_kernel(row_keys, row_values, cached_keys, cached_values, out_ref):
    size = row_keys.shape[1]
    blocks = row_keys.shape[0] // BLK
    for n in range(blocks + 1):
        keys, values = (row_keys, row_values) if n < blocks else (cached_keys, cached_values)
        rows = slice(n * BLK, (n + 1) * BLK) if n < blocks else slice(0, BLK)
        out_ref[n, :, :size] = keys[rows]
        out_ref[n, :, size:] = values[rows].T


def turn_kernel(size, q_ref, qt_ref):
    for j in range(qt_ref.shape[0]):
        for h in range(qt_ref.shape[2] // BLK):
            piece = q_ref[j * BLK : (j + 1) * BLK, h * size : (h + 1) * size]
            qt_ref[j, :, h * BLK : (h + 1) * BLK] = piece.T


def attend_kernel(scale, row_span, shape, stage, first_stage, last_stage, begin, blocks, pieces, *refs):
    table_hbm, bounds_hbm, qt_hbm = refs[:3]
    refs = refs[3:]
    piece_refs, refs = refs[:pieces], refs[pieces:]
    if not first_stage:
        acc_in, top_in, *refs = refs
    if last_stage:
        out_ref, *refs = refs
    else:
        acc_out, top_out, *refs = refs
    table, bounds_ref, qt_ref, kv_ref, acc_ref, top_ref, score_a, score_b, tile_row, tile_first, tile_kind, sems = refs
    size = qt_ref.shape[1]
    wide = qt_ref.shape[2]
    half = wide // 2
    heads = wide // BLK
    depth = TILE * BLK
    span = acc_ref.shape[1]
    total, width, many = shape
    counts_at = total * width
    bases_at = counts_at + total * many

    copies = [pltpu.make_async_copy(table_hbm, table, sems.at[0])]
    at = 0
    for piece in piece_refs:
        target = kv_ref.at[pl.ds(at, piece.shape[0])]
        copies.append(pltpu.make_async_copy(piece, target, sems.at[len(copies)]))
        at += piece.shape[0]
    copies.append(pltpu.make_async_copy(bounds_hbm, bounds_ref, sems.at[len(copies)]))
    copies.append(pltpu.make_async_copy(qt_hbm, qt_ref, sems.at[len(copies)]))
    if not first_stage:
        copies.append(pltpu.make_async_copy(acc_in.at[pl.ds(begin, blocks)], acc_ref, sems.at[len(copies)]))
        copies.append(pltpu.make_async_copy(top_in.at[pl.ds(begin, blocks)], top_ref, sems.at[len(copies)]))
    for copy in copies:
        copy.start()
    if first_stage:
        acc_ref[...] = jnp.zeros(acc_ref.shape, jnp.float32)
        top_ref[...] = jnp.full(top_ref.shape, LOWEST, jnp.float32)

    copies[0].wait()

    def list_row(j, t):
        here = counts_at + (begin + j) * many + 3 * stage
        offset, whole, seen = table[here], table[here + 1], table[here + 2]
        offset = offset + (begin + j) * width

        def list_tile(i, t):
            tile_row[t] = j
            tile_first[t] = offset + i * TILE
            tile_kind[t] = jnp.where(i * TILE + TILE <= whole, TILE + 1, jnp.minimum(seen - i * TILE, TILE))
            return t + 1

        return lax.fori_loop(0, (seen + (TILE - 1)) // TILE, list_tile, t)

    tiles = lax.fori_loop(0, blocks, list_row, 0)
    for n in range(2):
        tile_row[tiles + n] = 0
        tile_first[tiles + n] = 0
        tile_kind[tiles + n] = 0
    for copy in copies[1:]:
        copy.wait()

    ones = jnp.ones((span - size, depth), jnp.bfloat16)
    key_row = lax.broadcasted_iota(jnp.int32, (BLK, half), 0)

    def indices(t):
        first, kind = tile_first[t], tile_kind[t]
        return [jnp.where(n < kind, table[first + n], 0) for n in range(TILE)]

    def score(t, score_ref):
        keys = jnp.concatenate([kv_ref[index & 255, :, :size] for index in indices(t)], axis=0)
        j = tile_row[t] + begin
        for part in range(2):
            cols = slice(part * half, (part + 1) * half)
            score_ref[:, cols] = jnp.dot(keys, qt_ref[j, :, cols], preferred_element_type=jnp.float32)

    def fold(t, score_ref, masked):
        picked = indices(t)
        values = jnp.concatenate([kv_ref[index & 255, :, size:] for index in picked], axis=1)
        values = jnp.concatenate([values, ones], axis=0)
        j = tile_row[t]
        kind = tile_kind[t]
        for part in range(2):
            cols = slice(part * half, (part + 1) * half)
            if masked:
                shown = []
                for n, index in enumerate(picked):
                    base = jnp.where(n < kind, table[bases_at + (index >> 8)], FAR)
                    cached = base >= row_span
                    low = jnp.where(cached, bounds_ref[begin + j, 2:3, cols], bounds_ref[begin + j, 0:1, cols])
                    high = jnp.where(cached, bounds_ref[begin + j, 3:4, cols], bounds_ref[begin + j, 1:2, cols])
                    piece = score_ref[n * BLK : (n + 1) * BLK, cols]
                    shown.append(jnp.where((key_row >= low - base) & (key_row <= high - base), piece, UNSEEN))
                scores = jnp.concatenate(shown, axis=0)
            else:
                scores = score_ref[:, cols]
            old = top_ref[j, 0:1, cols]
            new = jnp.maximum(old, jnp.max(scores, axis=0, keepdims=True))
            weight = jnp.exp2(scores * scale - new * scale).astype(jnp.bfloat16)
            factor = jnp.exp2((old - new) * scale)
            top_ref[j, 0:1, cols] = new
            acc_ref[j, :, cols] = acc_ref[j, :, cols] * factor + jnp.dot(
                values, weight, preferred_element_type=jnp.float32
            )

    def step(t, here, there):
        plain = tile_kind[t] > TILE

        @pl.when(plain)
        def _():
            score(t + 1, there)
            fold(t, here, False)

        @pl.when(jnp.logical_not(plain))
        def _():
            score(t + 1, there)
            fold(t, here, True)

    def pair(i, _):
        step(2 * i, score_a, score_b)
        step(2 * i + 1, score_b, score_a)
        return 0

    @pl.when(tiles > 0)
    def _():
        score(0, score_a)
        lax.fori_loop(0, (tiles + 1) // 2, pair, 0)

    if last_stage:

        def finish(j, _):
            rows = pl.ds(pl.multiple_of(j * BLK, BLK), BLK)
            for h in range(heads):
                cols = slice(h * BLK, (h + 1) * BLK)
                result = acc_ref[j, :size, cols] / acc_ref[j, size : size + 1, cols]
                out_ref[rows, h * size : (h + 1) * size] = result.T.astype(out_ref.dtype)
            return 0

        lax.fori_loop(0, blocks, finish, 0)
    else:
        back = [
            pltpu.make_async_copy(acc_ref, acc_out, sems.at[0]),
            pltpu.make_async_copy(top_ref, top_out, sems.at[1]),
        ]
        for copy in back:
            copy.start()
        for copy in back:
            copy.wait()


def attend(qt, pieces, lists, stage, state, row_span, name, begin=0, blocks=None, last_stage=False):
    table, bounds, shape = lists
    total, size, wide = qt.shape
    blocks = total if blocks is None else blocks
    first_stage = state is None
    scale = 1.4426950408889634 / size**0.5
    span = size + 16
    vmem = pl.BlockSpec(memory_space=pltpu.VMEM)
    hbm = pl.BlockSpec(memory_space=pl.ANY)
    held = sum(piece.shape[0] for piece in pieces)
    tiles = blocks * (held // TILE) + 2
    if last_stage:
        out_shape = jax.ShapeDtypeStruct((blocks * BLK, wide // BLK * size), jnp.bfloat16)
        out_specs = vmem
    else:
        out_shape = (
            jax.ShapeDtypeStruct((total, span, wide), jnp.float32),
            jax.ShapeDtypeStruct((total, 8, wide), jnp.float32),
        )
        out_specs = (hbm, hbm)
    return pl.pallas_call(
        functools.partial(
            attend_kernel, scale, row_span, shape, stage, first_stage, last_stage, begin, blocks, len(pieces)
        ),
        out_shape=out_shape,
        in_specs=[hbm] * (3 + len(pieces) + (0 if first_stage else 2)),
        out_specs=out_specs,
        scratch_shapes=[
            pltpu.SMEM(table.shape, jnp.int32),
            pltpu.VMEM(bounds.shape, jnp.int32),
            pltpu.VMEM(qt.shape, jnp.bfloat16),
            pltpu.VMEM((held, BLK, 2 * size), jnp.bfloat16),
            pltpu.VMEM((blocks, span, wide), jnp.float32),
            pltpu.VMEM((blocks, 8, wide), jnp.float32),
            pltpu.VMEM((TILE * BLK, wide), jnp.float32),
            pltpu.VMEM((TILE * BLK, wide), jnp.float32),
            pltpu.SMEM((tiles,), jnp.int32),
            pltpu.SMEM((tiles,), jnp.int32),
            pltpu.SMEM((tiles,), jnp.int32),
            pltpu.SemaphoreType.DMA((len(pieces) + 5,)),
        ],
        compiler_params=pltpu.CompilerParams(vmem_limit_bytes=56 << 20),
        cost_estimate=pl.CostEstimate(flops=8 << 30, bytes_accessed=16 << 20, transcendentals=8 << 20),
        name=name,
    )(table, bounds, qt, *pieces, *(() if first_stage else state))


def plan(doc_ids, prefix_lens, block_order, mine, stage_of, place_of, heads):
    block_count = block_order.shape[0]
    rows = doc_ids.shape[0]
    shards = stage_of.shape[0]
    stages = 2
    inside = jnp.arange(BLK, dtype=jnp.int32)
    doc = doc_ids.reshape(block_count, BLK)[mine]
    position = mine[:, None] * BLK + inside[None, :]
    docs = jnp.arange(prefix_lens.shape[0], dtype=jnp.int32)
    doc_start = jnp.sum((doc_ids[None, :] < docs[:, None]).astype(jnp.int32), axis=1)
    prefix_end = jnp.cumsum(prefix_lens)
    prefix_start = prefix_end - prefix_lens
    chosen = doc[:, :, None] == docs[None, None, :]
    pick = lambda table: jnp.sum(jnp.where(chosen, table[None, None, :], 0), axis=2)
    low_row, high_row = pick(doc_start), position
    low_cached, high_cached = pick(prefix_start) + rows, pick(prefix_end) + (rows - 1)
    bounds = jnp.stack([low_row, high_row, low_cached, high_cached], axis=1)
    bounds = jnp.tile(bounds, (1, 2, heads)).astype(jnp.int32)
    row_base = block_order.reshape(shards, -1) * BLK
    cached_base = rows + jnp.arange(shards, dtype=jnp.int32)[:, None] * BLK
    base = jnp.concatenate([row_base, cached_base], axis=1).reshape(-1)
    first = base[None, :]
    last = first + (BLK - 1)
    cached = first >= rows
    ends = lambda array, at: array[:, at][:, None]
    seen = jnp.where(
        cached,
        (last >= ends(low_cached, 0)) & (first <= ends(high_cached, -1)),
        (last >= ends(low_row, 0)) & (first <= ends(high_row, -1)),
    )
    whole = jnp.where(
        cached,
        (first >= ends(low_cached, -1)) & (last <= ends(high_cached, 0)),
        (first >= ends(low_row, -1)) & (last <= ends(high_row, 0)),
    )
    unit = base.shape[0] // shards
    index = jnp.arange(base.shape[0], dtype=jnp.int32)
    spread = lambda array: jnp.broadcast_to(array[:, None], (shards, unit)).reshape(-1)
    stage = spread(stage_of)[None, :]
    slot = index * 256 + spread(place_of) * unit + index % unit
    key = jnp.where(seen, stage * (1 << 20) + jnp.where(whole, 0, 1 << 19) + slot[None, :], (1 << 24) + slot[None, :])
    order = lax.sort(key, dimension=1) & ((1 << 19) - 1)
    order = jnp.pad(order, ((0, 0), (0, TILE)))
    counts = []
    offset = jnp.zeros((mine.shape[0],), jnp.int32)
    for n in range(stages):
        here = stage == n
        many = jnp.sum(seen & here, axis=1).astype(jnp.int32)
        counts += [offset, jnp.sum(whole & seen & here, axis=1).astype(jnp.int32), many]
        offset = offset + many
    counts = jnp.stack(counts, axis=1)
    table = jnp.concatenate([order.reshape(-1), counts.reshape(-1), base])
    return table, bounds, (mine.shape[0], order.shape[1], counts.shape[1])


def around(first_axis, shift, n_x, n_y):
    pairs = []
    for x in range(n_x):
        for y in range(n_y):
            for core in range(2):
                along_x = (core == 0) == first_axis
                to = ((x + shift) % n_x, y) if along_x else (x, (y + shift) % n_y)
                pairs.append(((x * n_y + y) * 2 + core, (to[0] * n_y + to[1]) * 2 + core))
    return pairs


def on_device(
    queries,
    row_keys,
    row_values,
    cached_keys,
    cached_values,
    doc_ids,
    prefix_lens,
    block_order,
    out_weight,
):
    size = row_keys.shape[1]
    heads = queries.shape[1] // size
    local_blocks = queries.shape[0] // BLK
    n_x, n_y, n_z = lax.axis_size("x"), lax.axis_size("y"), lax.axis_size("z")
    x, y, core, z = (lax.axis_index(axis) for axis in ("x", "y", "core", "z"))
    rows = doc_ids.shape[0]
    shards = n_x * n_y * 2

    move = lambda array, first_axis, shift: lax.ppermute(array, CTX, around(first_axis, shift, n_x, n_y))
    swap = lambda array: lax.ppermute(array, "core", [(0, 1), (1, 0)])
    along_z = lambda array, shift: lax.ppermute(array, "z", [(i, (i + shift) % n_z) for i in range(n_z)])

    own = pl.pallas_call(
        pack_kernel,
        out_shape=jax.ShapeDtypeStruct((local_blocks + 1, BLK, 2 * size), jnp.bfloat16),
        cost_estimate=pl.CostEstimate(flops=0, bytes_accessed=4 << 20, transcendentals=0),
        name="pack",
    )(row_keys, row_values, cached_keys, cached_values)
    own, out_weight = lax.optimization_barrier((own, out_weight))
    right, left, far = move(own, True, 1), move(own, True, -1), move(own, True, 2)

    columns = out_weight.shape[1] // n_z
    depth = out_weight.shape[0]
    share = depth // 2
    half_for = lambda shift: lax.dynamic_slice(
        out_weight, (core * share, ((z + shift) % n_z) * columns), (share, columns)
    )
    given = [half_for(s) for s in (1, -1, 2)]
    got = [along_z(given[0], 1), along_z(given[1], -1)]
    one = jnp.concatenate([own, right], axis=0)
    one, got, left, far = lax.optimization_barrier((one, got, left, far))
    two = jnp.concatenate([left, far], axis=0)
    near = (move(one, False, 1), move(two, False, -1))
    next_near = (move(two, False, 1), move(one, False, -1))
    two, doc_ids, prefix_lens, block_order, queries = lax.optimization_barrier(
        (two, doc_ids, prefix_lens, block_order, queries)
    )

    shard = jnp.arange(shards, dtype=jnp.int32)
    shard_x, shard_y, shard_core = shard // (2 * n_y), shard // 2 % n_y, shard % 2
    apart_x, apart_y = (x - shard_x) % n_x, (y - shard_y) % n_y
    apart_first = jnp.where(shard_core == 0, apart_x, apart_y)
    apart_second = jnp.where(shard_core == 0, apart_y, apart_x)
    early = apart_first <= 1
    late = jnp.logical_not(early)
    same, facing = apart_second == 0, apart_second == 2
    soon = same | ((apart_second == 1) & early) | ((apart_second == 3) & late)
    stage_of = jnp.where(soon, 0, 1)
    piece_of = jnp.where(same, 0, 2) + late.astype(jnp.int32)
    piece_of = jnp.where(soon | facing, piece_of, early.astype(jnp.int32))
    along = jnp.where(early, apart_first, 3 - apart_first)
    place_of = jnp.where(shard_core == core, 0, 8) + 2 * piece_of + along
    mine = lax.dynamic_slice_in_dim(block_order, ((x * n_y + y) * 2 + core) * local_blocks, local_blocks, 0)
    table, bounds, shape = plan(doc_ids, prefix_lens, block_order, mine, stage_of, place_of, heads)
    qt = pl.pallas_call(
        functools.partial(turn_kernel, size),
        out_shape=jax.ShapeDtypeStruct((local_blocks, size, heads * BLK), jnp.bfloat16),
        cost_estimate=pl.CostEstimate(flops=0, bytes_accessed=4 << 20, transcendentals=0),
        name="turn",
    )(queries)

    lists = (table, bounds, shape)
    both = lambda arrays: tuple(arrays) + tuple(swap(array) for array in arrays)
    swapped = (swap(one), swap(two))
    near, swapped, qt, table, bounds = lax.optimization_barrier((near, swapped, qt, table, bounds))
    lists = (table, bounds, shape)
    across = (move(near[0], False, 1), move(near[1], False, -1))
    near_swapped = tuple(swap(array) for array in near)
    got = got + [along_z(given[2], 2)]
    state = attend(qt, (one, two) + near + swapped + near_swapped, lists, 0, None, rows, "attend_first")
    next_near, across, state, got = lax.optimization_barrier((next_near, across, state, got))
    final = next_near + across + tuple(swap(array) for array in next_near + across)
    part_blocks = local_blocks // 2
    part_rows = part_blocks * BLK
    parts = []
    for part in range(2):
        parts.append(
            attend(
                qt,
                final,
                lists,
                1,
                state,
                rows,
                "attend_last",
                begin=part * part_blocks,
                blocks=part_blocks,
                last_stage=True,
            )
        )
        if part == 0:
            first, state = lax.optimization_barrier((parts[0], state))
            parts[0] = first
    below, above = [along_z(parts[0], 1)], [along_z(parts[0], -1)]
    parts[1], below[0], above[0], got, out_weight = lax.optimization_barrier(
        (parts[1], below[0], above[0], got, out_weight)
    )
    below.append(along_z(parts[1], 1))
    above.append(along_z(parts[1], -1))
    got = jnp.concatenate(got, axis=0)
    other = swap(got)
    weight = jnp.zeros((n_z * depth, columns), out_weight.dtype)
    put = lambda array, piece, row: lax.dynamic_update_slice(array, piece, (row, 0))
    weight = put(weight, lax.dynamic_slice_in_dim(out_weight, z * columns, columns, 1), 0)
    for n in range(3):
        part = slice(n * share, (n + 1) * share)
        weight = put(weight, got[part], (n + 1) * depth + core * share)
        weight = put(weight, other[part], (n + 1) * depth + (1 - core) * share)
    below[1], above[1], weight = lax.optimization_barrier((below[1], above[1], weight))
    known = jnp.concatenate(
        [jnp.concatenate([parts[n], below[n], above[n]], axis=1) for n in range(2)], axis=0
    )
    partial = jnp.dot(known, weight[: 3 * depth], preferred_element_type=jnp.float32)
    opposite = jnp.concatenate([along_z(below[0], 1), along_z(above[1], -1)], axis=0)
    opposite, partial = lax.optimization_barrier((opposite, partial))
    rest = jnp.dot(opposite, weight[3 * depth :], preferred_element_type=jnp.float32)
    return (partial + rest).astype(jnp.bfloat16)


def solution(mesh):
    grid = Mesh(mesh.devices.reshape(4, 4, 2, mesh.shape["head"]), ("x", "y", "core", "z"))
    placed = (
        P(CTX, "z"),
        P(CTX, None),
        P(CTX, None),
        P(CTX, None),
        P(CTX, None),
        P(),
        P(),
        P(),
        P("z", None),
    )
    return jax.shard_map(
        on_device, mesh=grid, in_specs=placed, out_specs=P(CTX, "z"), check_vma=False
    )
```

```python
import functools

import jax
import jax.numpy as jnp
from jax import lax
from jax.experimental import pallas as pl
from jax.experimental.pallas import tpu as pltpu
from jax.sharding import Mesh
from jax.sharding import PartitionSpec as P

BLK = 128
TILE = 4
UNSEEN = -2e30
LOWEST = -1e30
FAR = 1 << 24
CTX = ("x", "y", "core")


def pack_kernel(row_keys, row_values, cached_keys, cached_values, out_ref):
    size = row_keys.shape[1]
    blocks = row_keys.shape[0] // BLK
    for n in range(blocks + 1):
        keys, values = (row_keys, row_values) if n < blocks else (cached_keys, cached_values)
        rows = slice(n * BLK, (n + 1) * BLK) if n < blocks else slice(0, BLK)
        out_ref[n, :, :size] = keys[rows]
        out_ref[n, :, size:] = values[rows].T


def turn_kernel(size, q_ref, qt_ref):
    for j in range(qt_ref.shape[0]):
        for h in range(qt_ref.shape[2] // BLK):
            piece = q_ref[j * BLK : (j + 1) * BLK, h * size : (h + 1) * size]
            qt_ref[j, :, h * BLK : (h + 1) * BLK] = piece.T


def attend_kernel(scale, row_span, shape, stage, first_stage, last_stage, begin, blocks, pieces, *refs):
    table_hbm, bounds_hbm, qt_hbm = refs[:3]
    refs = refs[3:]
    piece_refs, refs = refs[:pieces], refs[pieces:]
    if not first_stage:
        acc_in, top_in, *refs = refs
    if last_stage:
        out_ref, *refs = refs
    else:
        acc_out, top_out, *refs = refs
    table, bounds_ref, qt_ref, kv_ref, acc_ref, top_ref, score_a, score_b, tile_row, tile_first, tile_kind, sems, arrived = refs
    size = qt_ref.shape[1]
    wide = qt_ref.shape[2]
    half = wide // 2
    heads = wide // BLK
    depth = TILE * BLK
    span = acc_ref.shape[1]
    total, width, many = shape
    counts_at = total * width
    bases_at = counts_at + total * many

    copies = [pltpu.make_async_copy(table_hbm, table, sems.at[0])]
    copies.append(pltpu.make_async_copy(bounds_hbm, bounds_ref, sems.at[1]))
    copies.append(pltpu.make_async_copy(qt_hbm, qt_ref, sems.at[2]))
    if not first_stage:
        copies.append(pltpu.make_async_copy(acc_in.at[pl.ds(begin, blocks)], acc_ref, sems.at[3]))
        copies.append(pltpu.make_async_copy(top_in.at[pl.ds(begin, blocks)], top_ref, sems.at[4]))
    for copy in copies:
        copy.start()
    unit = min(piece.shape[0] for piece in piece_refs)
    units = [(piece, at) for piece in piece_refs for at in range(0, piece.shape[0], unit)]
    assert unit == 18

    def fetch(entry, slot, t):
        local = entry & 255
        which = (local * 3641) >> 16
        row = local - which * unit

        def start(low, high):
            if high - low == 1:
                piece, at = units[low]
                pltpu.make_async_copy(piece.at[at + row], kv_ref.at[slot], arrived.at[t]).start()
                return
            middle = (low + high) // 2
            pl.when(which < middle)(lambda: start(low, middle))
            pl.when(which >= middle)(lambda: start(middle, high))

        start(0, len(units))

    if first_stage:
        acc_ref[...] = jnp.zeros(acc_ref.shape, jnp.float32)
        top_ref[...] = jnp.full(top_ref.shape, LOWEST, jnp.float32)

    copies[0].wait()

    def list_row(j, t):
        here = counts_at + (begin + j) * many + 3 * stage
        offset, whole, seen = table[here], table[here + 1], table[here + 2]
        offset = offset + (begin + j) * width

        def list_tile(i, t):
            tile_row[t] = j
            tile_first[t] = offset + i * TILE
            tile_kind[t] = jnp.where(i * TILE + TILE <= whole, TILE + 1, jnp.minimum(seen - i * TILE, TILE))
            for n in range(TILE):
                fetch(table[offset + jnp.minimum(i * TILE + n, seen - 1)], t * TILE + n, t)
            return t + 1

        return lax.fori_loop(0, (seen + (TILE - 1)) // TILE, list_tile, t)

    tiles = lax.fori_loop(0, blocks, list_row, 0)
    for n in range(2):
        tile_row[tiles + n] = 0
        tile_first[tiles + n] = 0
        tile_kind[tiles + n] = 0
    for copy in copies[1:]:
        copy.wait()

    ones = jnp.ones((span - size, depth), jnp.bfloat16)
    key_row = lax.broadcasted_iota(jnp.int32, (BLK, half), 0)

    def await_tile(t):
        here = kv_ref.at[pl.ds(t * TILE, TILE)]
        pltpu.make_async_copy(units[0][0].at[pl.ds(0, TILE)], here, arrived.at[t]).wait()

    def slot_of(t):
        return jnp.where(tile_kind[t] > 0, t * TILE, 0)

    def score(t, score_ref, masked):
        slot = slot_of(t)
        keys = jnp.concatenate([kv_ref[slot + n, :, :size] for n in range(TILE)], axis=0)
        first = tile_first[t]
        j = tile_row[t] + begin
        kind = tile_kind[t]
        for part in range(2):
            cols = slice(part * half, (part + 1) * half)
            scores = jnp.dot(keys, qt_ref[j, :, cols], preferred_element_type=jnp.float32)
            if not masked:
                score_ref[:, cols] = scores
                continue
            for n in range(TILE):
                entry = jnp.where(n < kind, table[first + n], 0)
                base = jnp.where(n < kind, table[bases_at + (entry >> 8)], FAR)
                cached = base >= row_span
                low = jnp.where(cached, bounds_ref[j, 2:3, cols], bounds_ref[j, 0:1, cols]) - base
                high = jnp.where(cached, bounds_ref[j, 3:4, cols], bounds_ref[j, 1:2, cols]) - base
                keys_of = slice(n * BLK, (n + 1) * BLK)
                shown = (key_row >= low) & (key_row <= high)
                score_ref[keys_of, cols] = jnp.where(shown, scores[keys_of], UNSEEN)

    def fold(t, score_ref):
        slot = slot_of(t)
        values = jnp.concatenate([kv_ref[slot + n, :, size:] for n in range(TILE)], axis=1)
        values = jnp.concatenate([values, ones], axis=0)
        j = tile_row[t]
        for part in range(2):
            cols = slice(part * half, (part + 1) * half)
            scores = score_ref[:, cols]
            old = top_ref[j, 0:1, cols]
            new = jnp.maximum(old, jnp.max(scores, axis=0, keepdims=True))
            weight = jnp.exp2(scores * scale - new * scale).astype(jnp.bfloat16)
            factor = jnp.exp2((old - new) * scale)
            top_ref[j, 0:1, cols] = new
            acc_ref[j, :, cols] = acc_ref[j, :, cols] * factor + jnp.dot(
                values, weight, preferred_element_type=jnp.float32
            )

    def step(t, here, there):
        plain = tile_kind[t + 1] > TILE

        @pl.when(tile_kind[t + 1] > 0)
        def _():
            await_tile(t + 1)

        @pl.when(plain)
        def _():
            score(t + 1, there, False)
            fold(t, here)

        @pl.when(jnp.logical_not(plain))
        def _():
            score(t + 1, there, True)
            fold(t, here)

    def pair(i, _):
        step(2 * i, score_a, score_b)
        step(2 * i + 1, score_b, score_a)
        return 0

    @pl.when(tiles > 0)
    def _():
        await_tile(0)
        score(0, score_a, True)
        lax.fori_loop(0, (tiles + 1) // 2, pair, 0)

    if last_stage:

        def finish(j, _):
            rows = pl.ds(pl.multiple_of(j * BLK, BLK), BLK)
            for h in range(heads):
                cols = slice(h * BLK, (h + 1) * BLK)
                result = acc_ref[j, :size, cols] / acc_ref[j, size : size + 1, cols]
                out_ref[rows, h * size : (h + 1) * size] = result.T.astype(out_ref.dtype)
            return 0

        lax.fori_loop(0, blocks, finish, 0)
    else:
        back = [
            pltpu.make_async_copy(acc_ref, acc_out, sems.at[0]),
            pltpu.make_async_copy(top_ref, top_out, sems.at[1]),
        ]
        for copy in back:
            copy.start()
        for copy in back:
            copy.wait()


def attend(qt, pieces, lists, stage, state, row_span, name, begin=0, blocks=None, last_stage=False):
    table, bounds, shape = lists
    total, size, wide = qt.shape
    blocks = total if blocks is None else blocks
    first_stage = state is None
    scale = 1.4426950408889634 / size**0.5
    span = size + 16
    vmem = pl.BlockSpec(memory_space=pltpu.VMEM)
    hbm = pl.BlockSpec(memory_space=pl.ANY)
    held = sum(piece.shape[0] for piece in pieces)
    tiles = blocks * -(-min(held, 65) // TILE) + 2
    if last_stage:
        out_shape = jax.ShapeDtypeStruct((blocks * BLK, wide // BLK * size), jnp.bfloat16)
        out_specs = vmem
    else:
        out_shape = (
            jax.ShapeDtypeStruct((total, span, wide), jnp.float32),
            jax.ShapeDtypeStruct((total, 8, wide), jnp.float32),
        )
        out_specs = (hbm, hbm)
    return pl.pallas_call(
        functools.partial(
            attend_kernel, scale, row_span, shape, stage, first_stage, last_stage, begin, blocks, len(pieces)
        ),
        out_shape=out_shape,
        in_specs=[hbm] * (3 + len(pieces) + (0 if first_stage else 2)),
        out_specs=out_specs,
        scratch_shapes=[
            pltpu.SMEM(table.shape, jnp.int32),
            pltpu.VMEM(bounds.shape, jnp.int32),
            pltpu.VMEM(qt.shape, jnp.bfloat16),
            pltpu.VMEM((tiles * TILE, BLK, 2 * size), jnp.bfloat16),
            pltpu.VMEM((blocks, span, wide), jnp.float32),
            pltpu.VMEM((blocks, 8, wide), jnp.float32),
            pltpu.VMEM((TILE * BLK, wide), jnp.float32),
            pltpu.VMEM((TILE * BLK, wide), jnp.float32),
            pltpu.SMEM((tiles,), jnp.int32),
            pltpu.SMEM((tiles,), jnp.int32),
            pltpu.SMEM((tiles,), jnp.int32),
            pltpu.SemaphoreType.DMA((5,)),
            pltpu.SemaphoreType.DMA((tiles,)),
        ],
        compiler_params=pltpu.CompilerParams(vmem_limit_bytes=56 << 20),
        cost_estimate=pl.CostEstimate(flops=8 << 30, bytes_accessed=16 << 20, transcendentals=8 << 20),
        name=name,
    )(table, bounds, qt, *pieces, *(() if first_stage else state))


def plan(doc_ids, prefix_lens, block_order, mine, stage_of, place_of, heads):
    block_count = block_order.shape[0]
    rows = doc_ids.shape[0]
    shards = stage_of.shape[0]
    stages = 2
    inside = jnp.arange(BLK, dtype=jnp.int32)
    doc = doc_ids.reshape(block_count, BLK)[mine]
    position = mine[:, None] * BLK + inside[None, :]
    docs = jnp.arange(prefix_lens.shape[0], dtype=jnp.int32)
    doc_start = jnp.sum((doc_ids[None, :] < docs[:, None]).astype(jnp.int32), axis=1)
    prefix_end = jnp.cumsum(prefix_lens)
    prefix_start = prefix_end - prefix_lens
    chosen = doc[:, :, None] == docs[None, None, :]
    pick = lambda table: jnp.sum(jnp.where(chosen, table[None, None, :], 0), axis=2)
    low_row, high_row = pick(doc_start), position
    low_cached, high_cached = pick(prefix_start) + rows, pick(prefix_end) + (rows - 1)
    bounds = jnp.stack([low_row, high_row, low_cached, high_cached], axis=1)
    bounds = jnp.tile(bounds, (1, 2, heads)).astype(jnp.int32)
    row_base = block_order.reshape(shards, -1) * BLK
    cached_base = rows + jnp.arange(shards, dtype=jnp.int32)[:, None] * BLK
    base = jnp.concatenate([row_base, cached_base], axis=1).reshape(-1)
    first = base[None, :]
    last = first + (BLK - 1)
    cached = first >= rows
    ends = lambda array, at: array[:, at][:, None]
    seen = jnp.where(
        cached,
        (last >= ends(low_cached, 0)) & (first <= ends(high_cached, -1)),
        (last >= ends(low_row, 0)) & (first <= ends(high_row, -1)),
    )
    whole = jnp.where(
        cached,
        (first >= ends(low_cached, -1)) & (last <= ends(high_cached, 0)),
        (first >= ends(low_row, -1)) & (last <= ends(high_row, 0)),
    )
    unit = base.shape[0] // shards
    index = jnp.arange(base.shape[0], dtype=jnp.int32)
    spread = lambda array: jnp.broadcast_to(array[:, None], (shards, unit)).reshape(-1)
    stage = spread(stage_of)[None, :]
    slot = index * 256 + spread(place_of) * unit + index % unit
    key = jnp.where(seen, stage * (1 << 20) + jnp.where(whole, 0, 1 << 19) + slot[None, :], (1 << 24) + slot[None, :])
    order = lax.sort(key, dimension=1) & ((1 << 19) - 1)
    order = jnp.pad(order, ((0, 0), (0, TILE)))
    counts = []
    offset = jnp.zeros((mine.shape[0],), jnp.int32)
    for n in range(stages):
        here = stage == n
        many = jnp.sum(seen & here, axis=1).astype(jnp.int32)
        counts += [offset, jnp.sum(whole & seen & here, axis=1).astype(jnp.int32), many]
        offset = offset + many
    counts = jnp.stack(counts, axis=1)
    table = jnp.concatenate([order.reshape(-1), counts.reshape(-1), base])
    return table, bounds, (mine.shape[0], order.shape[1], counts.shape[1])


def around(first_axis, shift, n_x, n_y):
    pairs = []
    for x in range(n_x):
        for y in range(n_y):
            for core in range(2):
                along_x = (core == 0) == first_axis
                to = ((x + shift) % n_x, y) if along_x else (x, (y + shift) % n_y)
                pairs.append(((x * n_y + y) * 2 + core, (to[0] * n_y + to[1]) * 2 + core))
    return pairs


def on_device(
    queries,
    row_keys,
    row_values,
    cached_keys,
    cached_values,
    doc_ids,
    prefix_lens,
    block_order,
    out_weight,
):
    size = row_keys.shape[1]
    heads = queries.shape[1] // size
    local_blocks = queries.shape[0] // BLK
    n_x, n_y, n_z = lax.axis_size("x"), lax.axis_size("y"), lax.axis_size("z")
    x, y, core, z = (lax.axis_index(axis) for axis in ("x", "y", "core", "z"))
    rows = doc_ids.shape[0]
    shards = n_x * n_y * 2

    move = lambda array, first_axis, shift: lax.ppermute(array, CTX, around(first_axis, shift, n_x, n_y))
    swap = lambda array: lax.ppermute(array, "core", [(0, 1), (1, 0)])
    along_z = lambda array, shift: lax.ppermute(array, "z", [(i, (i + shift) % n_z) for i in range(n_z)])

    own = pl.pallas_call(
        pack_kernel,
        out_shape=jax.ShapeDtypeStruct((local_blocks + 1, BLK, 2 * size), jnp.bfloat16),
        cost_estimate=pl.CostEstimate(flops=0, bytes_accessed=4 << 20, transcendentals=0),
        name="pack",
    )(row_keys, row_values, cached_keys, cached_values)
    own, doc_ids, prefix_lens, block_order = lax.optimization_barrier(
        (own, doc_ids, prefix_lens, block_order)
    )
    right, left, far = move(own, True, 1), move(own, True, -1), move(own, True, 2)

    one = jnp.concatenate([own, right], axis=0)
    two = jnp.concatenate([left, far], axis=0)
    near = (move(one, False, 1), move(two, False, -1))

    shard = jnp.arange(shards, dtype=jnp.int32)
    shard_x, shard_y, shard_core = shard // (2 * n_y), shard // 2 % n_y, shard % 2
    apart_x, apart_y = (x - shard_x) % n_x, (y - shard_y) % n_y
    apart_first = jnp.where(shard_core == 0, apart_x, apart_y)
    apart_second = jnp.where(shard_core == 0, apart_y, apart_x)
    early = apart_first <= 1
    late = jnp.logical_not(early)
    same, facing = apart_second == 0, apart_second == 2
    soon = same | ((apart_second == 1) & early) | ((apart_second == 3) & late)
    stage_of = jnp.where(soon, 0, 1)
    piece_of = jnp.where(same, 0, 2) + late.astype(jnp.int32)
    piece_of = jnp.where(soon | facing, piece_of, early.astype(jnp.int32))
    along = jnp.where(early, apart_first, 3 - apart_first)
    place_of = jnp.where(shard_core == core, 0, 8) + 2 * piece_of + along
    mine = lax.dynamic_slice_in_dim(block_order, ((x * n_y + y) * 2 + core) * local_blocks, local_blocks, 0)
    table, bounds, shape = plan(doc_ids, prefix_lens, block_order, mine, stage_of, place_of, heads)
    one, two, table, bounds, out_weight, queries = lax.optimization_barrier(
        (one, two, table, bounds, out_weight, queries)
    )
    columns = out_weight.shape[1] // n_z
    depth = out_weight.shape[0]
    share = depth // 2
    half_for = lambda shift: lax.dynamic_slice(
        out_weight, (core * share, ((z + shift) % n_z) * columns), (share, columns)
    )
    given = [half_for(s) for s in (1, -1, 2)]
    got = [along_z(given[0], 1), along_z(given[1], -1)]
    qt = pl.pallas_call(
        functools.partial(turn_kernel, size),
        out_shape=jax.ShapeDtypeStruct((local_blocks, size, heads * BLK), jnp.bfloat16),
        cost_estimate=pl.CostEstimate(flops=0, bytes_accessed=4 << 20, transcendentals=0),
        name="turn",
    )(queries)

    lists = (table, bounds, shape)
    both = lambda arrays: tuple(arrays) + tuple(swap(array) for array in arrays)
    next_near = (move(two, False, 1), move(one, False, -1))
    swapped = (swap(jnp.concatenate([one, two], axis=0)),)
    near, swapped, qt, got = lax.optimization_barrier((near, swapped, qt, got))
    lists = (table, bounds, shape)
    across = (move(near[0], False, 1), move(near[1], False, -1))
    near_swapped = tuple(swap(array) for array in near)
    got = got + [along_z(given[2], 2)]
    state = attend(qt, (one, two) + near + swapped + near_swapped, lists, 0, None, rows, "attend_first")
    next_near, state, got = lax.optimization_barrier((next_near, state, got))
    next_swapped = tuple(swap(array) for array in next_near)
    next_swapped, across, state = lax.optimization_barrier((next_swapped, across, state))
    final = next_near + across + next_swapped + tuple(swap(array) for array in across)
    part_blocks = local_blocks // 2
    part_rows = part_blocks * BLK
    parts = []
    for part in range(2):
        parts.append(
            attend(
                qt,
                final,
                lists,
                1,
                state,
                rows,
                "attend_last",
                begin=part * part_blocks,
                blocks=part_blocks,
                last_stage=True,
            )
        )
        if part == 0:
            first, state = lax.optimization_barrier((parts[0], state))
            parts[0] = first
    below, above = [along_z(parts[0], 1)], [along_z(parts[0], -1)]
    below.append(along_z(parts[1], 1))
    above.append(along_z(parts[1], -1))
    parts[1], below[0], above[0], got, out_weight = lax.optimization_barrier(
        (parts[1], below[0], above[0], got, out_weight)
    )
    got = jnp.concatenate(got, axis=0)
    other = swap(got)
    weight = jnp.zeros((n_z * depth, columns), out_weight.dtype)
    put = lambda array, piece, row: lax.dynamic_update_slice(array, piece, (row, 0))
    weight = put(weight, lax.dynamic_slice_in_dim(out_weight, z * columns, columns, 1), 0)
    for n in range(3):
        part = slice(n * share, (n + 1) * share)
        weight = put(weight, got[part], (n + 1) * depth + core * share)
        weight = put(weight, other[part], (n + 1) * depth + (1 - core) * share)
    below[1], above[1], weight = lax.optimization_barrier((below[1], above[1], weight))
    known = jnp.concatenate(
        [jnp.concatenate([parts[n], below[n], above[n]], axis=1) for n in range(2)], axis=0
    )
    partial = jnp.dot(known, weight[: 3 * depth], preferred_element_type=jnp.float32)
    opposite = jnp.concatenate([along_z(below[0], 1), along_z(above[1], -1)], axis=0)
    opposite, partial = lax.optimization_barrier((opposite, partial))
    rest = jnp.dot(opposite, weight[3 * depth :], preferred_element_type=jnp.float32)
    return (partial + rest).astype(jnp.bfloat16)


def solution(mesh):
    grid = Mesh(mesh.devices.reshape(4, 4, 2, mesh.shape["head"]), ("x", "y", "core", "z"))
    placed = (
        P(CTX, "z"),
        P(CTX, None),
        P(CTX, None),
        P(CTX, None),
        P(CTX, None),
        P(),
        P(),
        P(),
        P("z", None),
    )
    return jax.shard_map(
        on_device, mesh=grid, in_specs=placed, out_specs=P(CTX, "z"), check_vma=False
    )
```

```python
import functools

import jax
import jax.numpy as jnp
from jax import lax
from jax.experimental import pallas as pl
from jax.experimental.pallas import tpu as pltpu
from jax.sharding import Mesh
from jax.sharding import PartitionSpec as P

BLK = 128
TILE = 4
UNSEEN = -2e30
LOWEST = -1e30
FAR = 1 << 24
CTX = ("x", "y", "core")


def pack_kernel(row_keys, row_values, cached_keys, cached_values, out_ref):
    size = row_keys.shape[1]
    blocks = row_keys.shape[0] // BLK
    for n in range(blocks + 1):
        keys, values = (row_keys, row_values) if n < blocks else (cached_keys, cached_values)
        rows = slice(n * BLK, (n + 1) * BLK) if n < blocks else slice(0, BLK)
        out_ref[n, :, :size] = keys[rows]
        out_ref[n, :, size:] = values[rows].T


def turn_kernel(size, q_ref, qt_ref):
    for j in range(qt_ref.shape[0]):
        for h in range(qt_ref.shape[2] // BLK):
            piece = q_ref[j * BLK : (j + 1) * BLK, h * size : (h + 1) * size]
            qt_ref[j, :, h * BLK : (h + 1) * BLK] = piece.T


def attend_kernel(scale, row_span, shape, stage, first_stage, last_stage, begin, blocks, pieces, *refs):
    table_hbm, bounds_hbm, qt_hbm = refs[:3]
    refs = refs[3:]
    piece_refs, refs = refs[:pieces], refs[pieces:]
    if not first_stage:
        acc_in, top_in, *refs = refs
    if last_stage:
        out_ref, *refs = refs
    else:
        acc_out, top_out, *refs = refs
    table, bounds_ref, qt_ref, kv_ref, acc_ref, top_ref, score_a, score_b, tile_row, tile_first, tile_kind, sems, arrived = refs
    size = qt_ref.shape[1]
    wide = qt_ref.shape[2]
    half = wide // 2
    heads = wide // BLK
    depth = TILE * BLK
    span = acc_ref.shape[1]
    total, width, many = shape
    counts_at = total * width
    bases_at = counts_at + total * many

    copies = [pltpu.make_async_copy(table_hbm, table, sems.at[0])]
    copies.append(pltpu.make_async_copy(bounds_hbm, bounds_ref, sems.at[1]))
    copies.append(pltpu.make_async_copy(qt_hbm, qt_ref, sems.at[2]))
    if not first_stage:
        copies.append(pltpu.make_async_copy(acc_in.at[pl.ds(begin, blocks)], acc_ref, sems.at[3]))
        copies.append(pltpu.make_async_copy(top_in.at[pl.ds(begin, blocks)], top_ref, sems.at[4]))
    for copy in copies:
        copy.start()
    unit = min(piece.shape[0] for piece in piece_refs)
    units = [(piece, at) for piece in piece_refs for at in range(0, piece.shape[0], unit)]
    assert unit == 18

    def fetch(entry, slot, t):
        local = entry & 255
        which = (local * 3641) >> 16
        row = local - which * unit

        def start(low, high):
            if high - low == 1:
                piece, at = units[low]
                pltpu.make_async_copy(piece.at[at + row], kv_ref.at[slot], arrived.at[t]).start()
                return
            middle = (low + high) // 2
            pl.when(which < middle)(lambda: start(low, middle))
            pl.when(which >= middle)(lambda: start(middle, high))

        start(0, len(units))

    if first_stage:
        acc_ref[...] = jnp.zeros(acc_ref.shape, jnp.float32)
        top_ref[...] = jnp.full(top_ref.shape, LOWEST, jnp.float32)

    copies[0].wait()

    def list_row(j, t):
        here = counts_at + (begin + j) * many + 3 * stage
        offset, whole, seen = table[here], table[here + 1], table[here + 2]
        offset = offset + (begin + j) * width

        def list_tile(i, t):
            tile_row[t] = j
            tile_first[t] = offset + i * TILE
            tile_kind[t] = jnp.where(i * TILE + TILE <= whole, TILE + 1, jnp.minimum(seen - i * TILE, TILE))
            for n in range(TILE):
                fetch(table[offset + jnp.minimum(i * TILE + n, seen - 1)], t * TILE + n, t)
            return t + 1

        return lax.fori_loop(0, (seen + (TILE - 1)) // TILE, list_tile, t)

    tiles = lax.fori_loop(0, blocks, list_row, 0)
    for n in range(2):
        tile_row[tiles + n] = 0
        tile_first[tiles + n] = 0
        tile_kind[tiles + n] = 0
    for copy in copies[1:]:
        copy.wait()

    ones = jnp.ones((span - size, depth), jnp.bfloat16)
    key_row = lax.broadcasted_iota(jnp.int32, (BLK, half), 0)

    def await_tile(t):
        here = kv_ref.at[pl.ds(t * TILE, TILE)]
        pltpu.make_async_copy(units[0][0].at[pl.ds(0, TILE)], here, arrived.at[t]).wait()

    def slot_of(t):
        return jnp.where(tile_kind[t] > 0, t * TILE, 0)

    def score(t, score_ref, masked):
        slot = slot_of(t)
        keys = jnp.concatenate([kv_ref[slot + n, :, :size] for n in range(TILE)], axis=0)
        first = tile_first[t]
        j = tile_row[t] + begin
        kind = tile_kind[t]
        for part in range(2):
            cols = slice(part * half, (part + 1) * half)
            scores = jnp.dot(keys, qt_ref[j, :, cols], preferred_element_type=jnp.float32)
            if not masked:
                score_ref[:, cols] = scores
                continue
            for n in range(TILE):
                entry = jnp.where(n < kind, table[first + n], 0)
                base = jnp.where(n < kind, table[bases_at + (entry >> 8)], FAR)
                cached = base >= row_span
                low = jnp.where(cached, bounds_ref[j, 2:3, cols], bounds_ref[j, 0:1, cols]) - base
                high = jnp.where(cached, bounds_ref[j, 3:4, cols], bounds_ref[j, 1:2, cols]) - base
                keys_of = slice(n * BLK, (n + 1) * BLK)
                shown = (key_row >= low) & (key_row <= high)
                score_ref[keys_of, cols] = jnp.where(shown, scores[keys_of], UNSEEN)

    def fold(t, score_ref):
        slot = slot_of(t)
        values = jnp.concatenate([kv_ref[slot + n, :, size:] for n in range(TILE)], axis=1)
        values = jnp.concatenate([values, ones], axis=0)
        j = tile_row[t]
        for part in range(2):
            cols = slice(part * half, (part + 1) * half)
            scores = score_ref[:, cols]
            old = top_ref[j, 0:1, cols]
            new = jnp.maximum(old, jnp.max(scores, axis=0, keepdims=True))
            weight = jnp.exp2(scores * scale - new * scale).astype(jnp.bfloat16)
            factor = jnp.exp2((old - new) * scale)
            top_ref[j, 0:1, cols] = new
            acc_ref[j, :, cols] = acc_ref[j, :, cols] * factor + jnp.dot(
                values, weight, preferred_element_type=jnp.float32
            )

    def step(t, here, there):
        plain = tile_kind[t + 1] > TILE

        @pl.when(tile_kind[t + 1] > 0)
        def _():
            await_tile(t + 1)

        @pl.when(plain)
        def _():
            score(t + 1, there, False)
            fold(t, here)

        @pl.when(jnp.logical_not(plain))
        def _():
            score(t + 1, there, True)
            fold(t, here)

    def pair(i, _):
        step(2 * i, score_a, score_b)
        step(2 * i + 1, score_b, score_a)
        return 0

    @pl.when(tiles > 0)
    def _():
        await_tile(0)
        score(0, score_a, True)
        lax.fori_loop(0, (tiles + 1) // 2, pair, 0)

    if last_stage:

        def finish(j, _):
            rows = pl.ds(pl.multiple_of(j * BLK, BLK), BLK)
            for h in range(heads):
                cols = slice(h * BLK, (h + 1) * BLK)
                result = acc_ref[j, :size, cols] / acc_ref[j, size : size + 1, cols]
                out_ref[rows, h * size : (h + 1) * size] = result.T.astype(out_ref.dtype)
            return 0

        lax.fori_loop(0, blocks, finish, 0)
    else:
        back = [
            pltpu.make_async_copy(acc_ref, acc_out, sems.at[0]),
            pltpu.make_async_copy(top_ref, top_out, sems.at[1]),
        ]
        for copy in back:
            copy.start()
        for copy in back:
            copy.wait()


def attend(qt, pieces, lists, stage, state, row_span, name, begin=0, blocks=None, last_stage=False):
    table, bounds, shape = lists
    total, size, wide = qt.shape
    blocks = total if blocks is None else blocks
    first_stage = state is None
    scale = 1.4426950408889634 / size**0.5
    span = size + 16
    vmem = pl.BlockSpec(memory_space=pltpu.VMEM)
    hbm = pl.BlockSpec(memory_space=pl.ANY)
    held = sum(piece.shape[0] for piece in pieces)
    tiles = blocks * -(-min(held, 65) // TILE) + 2
    if last_stage:
        out_shape = jax.ShapeDtypeStruct((blocks * BLK, wide // BLK * size), jnp.bfloat16)
        out_specs = vmem
    else:
        out_shape = (
            jax.ShapeDtypeStruct((total, span, wide), jnp.float32),
            jax.ShapeDtypeStruct((total, 8, wide), jnp.float32),
        )
        out_specs = (hbm, hbm)
    return pl.pallas_call(
        functools.partial(
            attend_kernel, scale, row_span, shape, stage, first_stage, last_stage, begin, blocks, len(pieces)
        ),
        out_shape=out_shape,
        in_specs=[hbm] * (3 + len(pieces) + (0 if first_stage else 2)),
        out_specs=out_specs,
        scratch_shapes=[
            pltpu.SMEM(table.shape, jnp.int32),
            pltpu.VMEM(bounds.shape, jnp.int32),
            pltpu.VMEM(qt.shape, jnp.bfloat16),
            pltpu.VMEM((tiles * TILE, BLK, 2 * size), jnp.bfloat16),
            pltpu.VMEM((blocks, span, wide), jnp.float32),
            pltpu.VMEM((blocks, 8, wide), jnp.float32),
            pltpu.VMEM((TILE * BLK, wide), jnp.float32),
            pltpu.VMEM((TILE * BLK, wide), jnp.float32),
            pltpu.SMEM((tiles,), jnp.int32),
            pltpu.SMEM((tiles,), jnp.int32),
            pltpu.SMEM((tiles,), jnp.int32),
            pltpu.SemaphoreType.DMA((5,)),
            pltpu.SemaphoreType.DMA((tiles,)),
        ],
        compiler_params=pltpu.CompilerParams(vmem_limit_bytes=56 << 20),
        cost_estimate=pl.CostEstimate(flops=8 << 30, bytes_accessed=16 << 20, transcendentals=8 << 20),
        name=name,
    )(table, bounds, qt, *pieces, *(() if first_stage else state))


def plan(doc_ids, prefix_lens, block_order, mine, stage_of, place_of, heads):
    block_count = block_order.shape[0]
    rows = doc_ids.shape[0]
    shards = stage_of.shape[0]
    stages = 2
    inside = jnp.arange(BLK, dtype=jnp.int32)
    doc = doc_ids.reshape(block_count, BLK)[mine]
    position = mine[:, None] * BLK + inside[None, :]
    docs = jnp.arange(prefix_lens.shape[0], dtype=jnp.int32)
    doc_start = jnp.sum((doc_ids[None, :] < docs[:, None]).astype(jnp.int32), axis=1)
    prefix_end = jnp.cumsum(prefix_lens)
    prefix_start = prefix_end - prefix_lens
    chosen = doc[:, :, None] == docs[None, None, :]
    pick = lambda table: jnp.sum(jnp.where(chosen, table[None, None, :], 0), axis=2)
    low_row, high_row = pick(doc_start), position
    low_cached, high_cached = pick(prefix_start) + rows, pick(prefix_end) + (rows - 1)
    bounds = jnp.stack([low_row, high_row, low_cached, high_cached], axis=1)
    bounds = jnp.tile(bounds, (1, 2, heads)).astype(jnp.int32)
    row_base = block_order.reshape(shards, -1) * BLK
    cached_base = rows + jnp.arange(shards, dtype=jnp.int32)[:, None] * BLK
    base = jnp.concatenate([row_base, cached_base], axis=1).reshape(-1)
    first = base[None, :]
    last = first + (BLK - 1)
    cached = first >= rows
    ends = lambda array, at: array[:, at][:, None]
    seen = jnp.where(
        cached,
        (last >= ends(low_cached, 0)) & (first <= ends(high_cached, -1)),
        (last >= ends(low_row, 0)) & (first <= ends(high_row, -1)),
    )
    whole = jnp.where(
        cached,
        (first >= ends(low_cached, -1)) & (last <= ends(high_cached, 0)),
        (first >= ends(low_row, -1)) & (last <= ends(high_row, 0)),
    )
    unit = base.shape[0] // shards
    index = jnp.arange(base.shape[0], dtype=jnp.int32)
    spread = lambda array: jnp.broadcast_to(array[:, None], (shards, unit)).reshape(-1)
    stage = spread(stage_of)[None, :]
    slot = index * 256 + spread(place_of) * unit + index % unit
    key = jnp.where(seen, stage * (1 << 20) + jnp.where(whole, 0, 1 << 19) + slot[None, :], (1 << 24) + slot[None, :])
    order = lax.sort(key, dimension=1) & ((1 << 19) - 1)
    order = jnp.pad(order, ((0, 0), (0, TILE)))
    counts = []
    offset = jnp.zeros((mine.shape[0],), jnp.int32)
    for n in range(stages):
        here = stage == n
        many = jnp.sum(seen & here, axis=1).astype(jnp.int32)
        counts += [offset, jnp.sum(whole & seen & here, axis=1).astype(jnp.int32), many]
        offset = offset + many
    counts = jnp.stack(counts, axis=1)
    table = jnp.concatenate([order.reshape(-1), counts.reshape(-1), base])
    return table, bounds, (mine.shape[0], order.shape[1], counts.shape[1])


def around(first_axis, shift, n_x, n_y):
    pairs = []
    for x in range(n_x):
        for y in range(n_y):
            for core in range(2):
                along_x = (core == 0) == first_axis
                to = ((x + shift) % n_x, y) if along_x else (x, (y + shift) % n_y)
                pairs.append(((x * n_y + y) * 2 + core, (to[0] * n_y + to[1]) * 2 + core))
    return pairs


def on_device(
    queries,
    row_keys,
    row_values,
    cached_keys,
    cached_values,
    doc_ids,
    prefix_lens,
    block_order,
    out_weight,
):
    size = row_keys.shape[1]
    heads = queries.shape[1] // size
    local_blocks = queries.shape[0] // BLK
    n_x, n_y, n_z = lax.axis_size("x"), lax.axis_size("y"), lax.axis_size("z")
    x, y, core, z = (lax.axis_index(axis) for axis in ("x", "y", "core", "z"))
    rows = doc_ids.shape[0]
    shards = n_x * n_y * 2

    move = lambda array, first_axis, shift: lax.ppermute(array, CTX, around(first_axis, shift, n_x, n_y))
    swap = lambda array: lax.ppermute(array, "core", [(0, 1), (1, 0)])
    along_z = lambda array, shift: lax.ppermute(array, "z", [(i, (i + shift) % n_z) for i in range(n_z)])

    own = pl.pallas_call(
        pack_kernel,
        out_shape=jax.ShapeDtypeStruct((local_blocks + 1, BLK, 2 * size), jnp.bfloat16),
        cost_estimate=pl.CostEstimate(flops=0, bytes_accessed=4 << 20, transcendentals=0),
        name="pack",
    )(row_keys, row_values, cached_keys, cached_values)
    own, doc_ids, prefix_lens, block_order = lax.optimization_barrier(
        (own, doc_ids, prefix_lens, block_order)
    )
    right, left, far = move(own, True, 1), move(own, True, -1), move(own, True, 2)

    one = jnp.concatenate([own, right], axis=0)
    two = jnp.concatenate([left, far], axis=0)
    near = (move(one, False, 1), move(two, False, -1))

    shard = jnp.arange(shards, dtype=jnp.int32)
    shard_x, shard_y, shard_core = shard // (2 * n_y), shard // 2 % n_y, shard % 2
    apart_x, apart_y = (x - shard_x) % n_x, (y - shard_y) % n_y
    apart_first = jnp.where(shard_core == 0, apart_x, apart_y)
    apart_second = jnp.where(shard_core == 0, apart_y, apart_x)
    early = apart_first <= 1
    late = jnp.logical_not(early)
    same, facing = apart_second == 0, apart_second == 2
    soon = same | ((apart_second == 1) & early) | ((apart_second == 3) & late)
    stage_of = jnp.where(soon, 0, 1)
    piece_of = jnp.where(same, 0, 2) + late.astype(jnp.int32)
    piece_of = jnp.where(soon | facing, piece_of, early.astype(jnp.int32))
    along = jnp.where(early, apart_first, 3 - apart_first)
    place_of = jnp.where(shard_core == core, 0, 8) + 2 * piece_of + along
    mine = lax.dynamic_slice_in_dim(block_order, ((x * n_y + y) * 2 + core) * local_blocks, local_blocks, 0)
    table, bounds, shape = plan(doc_ids, prefix_lens, block_order, mine, stage_of, place_of, heads)
    one, two, table, bounds, out_weight, queries = lax.optimization_barrier(
        (one, two, table, bounds, out_weight, queries)
    )
    columns = out_weight.shape[1] // n_z
    depth = out_weight.shape[0]
    share = depth // 2
    half_for = lambda shift: lax.dynamic_slice(
        out_weight, (core * share, ((z + shift) % n_z) * columns), (share, columns)
    )
    given = [half_for(s) for s in (1, -1, 2)]
    got = [along_z(given[0], 1), along_z(given[1], -1)]
    qt = pl.pallas_call(
        functools.partial(turn_kernel, size),
        out_shape=jax.ShapeDtypeStruct((local_blocks, size, heads * BLK), jnp.bfloat16),
        cost_estimate=pl.CostEstimate(flops=0, bytes_accessed=4 << 20, transcendentals=0),
        name="turn",
    )(queries)

    lists = (table, bounds, shape)
    both = lambda arrays: tuple(arrays) + tuple(swap(array) for array in arrays)
    next_near = (move(two, False, 1), move(one, False, -1))
    swapped = (swap(jnp.concatenate([one, two], axis=0)),)
    near, swapped, qt, got = lax.optimization_barrier((near, swapped, qt, got))
    lists = (table, bounds, shape)
    across = (move(near[0], False, 1), move(near[1], False, -1))
    near_swapped = tuple(swap(array) for array in near)
    got = got + [along_z(given[2], 2)]
    state = attend(qt, (one, two) + near + swapped + near_swapped, lists, 0, None, rows, "attend_first")
    next_near, state, got = lax.optimization_barrier((next_near, state, got))
    next_swapped = tuple(swap(array) for array in next_near)
    next_swapped, across, state = lax.optimization_barrier((next_swapped, across, state))
    final = next_near + across + next_swapped + tuple(swap(array) for array in across)
    part_blocks = local_blocks // 2
    part_rows = part_blocks * BLK
    parts = []
    for part in range(2):
        parts.append(
            attend(
                qt,
                final,
                lists,
                1,
                state,
                rows,
                "attend_last",
                begin=part * part_blocks,
                blocks=part_blocks,
                last_stage=True,
            )
        )
        if part == 0:
            first, state = lax.optimization_barrier((parts[0], state))
            parts[0] = first
    below, above = [along_z(parts[0], 1)], [along_z(parts[0], -1)]
    below.append(along_z(parts[1], 1))
    above.append(along_z(parts[1], -1))
    parts[1], below[0], above[0], got, out_weight = lax.optimization_barrier(
        (parts[1], below[0], above[0], got, out_weight)
    )
    got = jnp.concatenate(got, axis=0)
    other = swap(got)
    weight = jnp.zeros((n_z * depth, columns), out_weight.dtype)
    put = lambda array, piece, row: lax.dynamic_update_slice(array, piece, (row, 0))
    weight = put(weight, lax.dynamic_slice_in_dim(out_weight, z * columns, columns, 1), 0)
    for n in range(3):
        part = slice(n * share, (n + 1) * share)
        weight = put(weight, got[part], (n + 1) * depth + core * share)
        weight = put(weight, other[part], (n + 1) * depth + (1 - core) * share)
    below[1], above[1], weight = lax.optimization_barrier((below[1], above[1], weight))
    known = jnp.concatenate(
        [jnp.concatenate([parts[n], below[n], above[n]], axis=1) for n in range(2)], axis=0
    )
    partial = jnp.dot(known, weight[: 3 * depth], preferred_element_type=jnp.float32)
    out = partial.astype(jnp.bfloat16)
    for n, opposite in enumerate((along_z(below[0], 1), along_z(above[1], -1))):
        opposite, partial, out = lax.optimization_barrier((opposite, partial, out))
        rest = jnp.dot(opposite, weight[3 * depth :], preferred_element_type=jnp.float32)
        known_rows = lax.slice_in_dim(partial, n * part_rows, (n + 1) * part_rows, axis=0)
        out = lax.dynamic_update_slice(out, (known_rows + rest).astype(jnp.bfloat16), (n * part_rows, 0))
    return out


def solution(mesh):
    grid = Mesh(mesh.devices.reshape(4, 4, 2, mesh.shape["head"]), ("x", "y", "core", "z"))
    placed = (
        P(CTX, "z"),
        P(CTX, None),
        P(CTX, None),
        P(CTX, None),
        P(CTX, None),
        P(),
        P(),
        P(),
        P("z", None),
    )
    return jax.shard_map(
        on_device, mesh=grid, in_specs=placed, out_specs=P(CTX, "z"), check_vma=False
    )
```
